32 devices in a mesh: dom: 4 (over x, core), st: 8 (over z, y).
Axes of the slice: x: 2, y: 2, z: 4, core: 2. Of those that a mesh axis runs over, the one named last changes fastest.
Arguments:
- orbitals: bfloat16 [512, 256, 1024], P('st', 'dom'), may hold values from -6 to 6
- potential: bfloat16 [256, 1024], P('dom'), may hold values from -0.5 to 0.5
- rotation: bfloat16 [512, 512], P('st'), may hold values from -0.25 to 0.25
Outputs:
- rotated: bfloat16 [512, 262144], P(None, ('dom', 'st'))
The draws below stay inside these ranges and needn't reach their ends.
All inputs are finite; a program needn't handle non-finite values.
Results may differ from the reference program's by a relative error of at most 0.0049.
Values may be sent and summed in bfloat16 or wider, within the bound.
A program may use at most 128 MiB of HBM per device.

```python
import jax
import jax.numpy as jnp
from jax import lax

STATES = 512
DEGREE = 4
NY = 32
NZ = 32
NX = 256


def block_scale(own_key, dims, cuts, low, high):
    gain = 1.0
    for dim, parts in cuts:
        heights = jax.random.uniform(jax.random.fold_in(jax.random.fold_in(own_key, 6), dim), (parts,), jnp.float32, low / len(cuts), high / len(cuts))
        gain = gain * jnp.repeat(jnp.exp(heights), dims[dim] // parts).reshape((-1,) + (1,) * (len(dims) - 1 - dim))
    return gain


def centred(stream_key, extent, scale, most, shards=(), dtype=jnp.bfloat16):
    array = scale * jax.random.normal(stream_key, extent, jnp.float32)
    if shards:
        array = array * block_scale(stream_key, extent, shards, -0.22, 0.18)
    return jnp.clip(array, -most, most).astype(dtype)


def setup_inputs(seed: int = 0) -> dict:
    keys = jax.random.split(jax.random.key(seed), 4)
    orbitals = centred(keys[0], (STATES, NX, NY * NZ), 1.0, 6.0, ((0, 8), (1, 4)))
    potential = jnp.clip(jax.random.uniform(keys[1], (NX, NY * NZ), jnp.float32, -0.5, 0.5) * block_scale(keys[1], (NX, NY * NZ), ((0, 4),), -0.4, 0.0), -0.5, 0.5).astype(jnp.bfloat16)
    rotation = centred(keys[2], (STATES, STATES), STATES ** -0.5, 0.25, ((0, 8),))
    return {"orbitals": orbitals, "potential": potential, "rotation": rotation}


cheb_shift = 3.75
cheb_scale = 3.25


def neighbour_sum(center, nz_count):
    row_width = center.shape[2]
    z_position = lax.broadcasted_iota(jnp.int32, (1, 1, row_width), 2) % nz_count
    padded = jnp.pad(center, ((0, 0), (0, 0), (nz_count, nz_count)))
    along_y = padded[:, :, 2 * nz_count:] + padded[:, :, :row_width]
    upper_z = jnp.where(z_position < nz_count - 1, padded[:, :, nz_count + 1:nz_count + 1 + row_width], 0.0)
    lower_z = jnp.where(z_position > 0, padded[:, :, nz_count - 1:nz_count - 1 + row_width], 0.0)
    return along_y + upper_z + lower_z


def hamiltonian(padded_x, local_pot, nz_count):
    center = padded_x[:, 1:-1]
    beside = padded_x[:, 2:] + padded_x[:, :-2] + neighbour_sum(center, nz_count)
    return (3.0 + local_pot) * center - 0.5 * beside


def chebyshev(start, apply_fn, degree):
    previous = start
    current = (apply_fn(start) - cheb_shift * start) / cheb_scale
    for filter_order in range(1, degree):
        following = 2.0 * (apply_fn(current) - cheb_shift * current) / cheb_scale - previous
        previous = current
        current = following
    return current


def reference(orbitals, potential, rotation):
    local_pot = potential.astype(jnp.float32)

    def apply_fn(state_field):
        return hamiltonian(jnp.pad(state_field, ((0, 0), (1, 1), (0, 0))), local_pot, NZ)

    def filter_block(block):
        return chebyshev(block.astype(jnp.float32), apply_fn, DEGREE).astype(jnp.bfloat16)

    filtered = lax.map(filter_block, orbitals.reshape(STATES // 16, 16, NX, NY * NZ))
    filtered = filtered.reshape(STATES, NX * NY * NZ)

    def rotate_block(rows):
        return jnp.dot(rows, filtered, preferred_element_type=jnp.float32).astype(jnp.bfloat16)

    rotated = lax.map(rotate_block, rotation.reshape(STATES // 16, 16, STATES))
    return rotated.reshape(STATES, NX * NY * NZ)
```

```python
import functools

import jax
import jax.numpy as jnp
from jax import lax
from jax.experimental import pallas as pl
from jax.experimental.pallas import tpu as pltpu
from jax.sharding import PartitionSpec as P

DEGREE = 4
NZ = 32
LANES = 128
ROWS = 16
MESH = pl.DeviceIdType.MESH

cheb_shift = 3.75
cheb_scale = 3.25


def filter_kernel(
    n_dom, n_st, parts,
    orb, pot, rot,
    gathered, rot_full,
    raw, halo, pot_v, pot_halo, alpha, y0, y1, y2, y3, stage,
    load_sem, pot_sem, halo_send, halo_recv, ph_send, ph_recv,
    send_sem, recv_sem, own_sem, r_send, r_recv, r_own, r2_send, r2_recv,
):
    dom = lax.axis_index("dom")
    me = lax.axis_index("st")
    states, planes, width = orb.shape
    chunks = states // ROWS
    block = planes // n_st
    half = n_st // 2
    cols = width // LANES
    part_rows = states // parts
    fields = (y0, y1, y2, y3)

    def load(c):
        return pltpu.make_async_copy(
            orb.at[pl.ds(c * ROWS, ROWS)], raw.at[pl.ds(c * ROWS, ROWS)], load_sem.at[c]
        )

    for c in range(chunks):
        load(c).start()
    pot_copy = pltpu.make_async_copy(pot, pot_v, pot_sem)
    pot_copy.start()

    barrier = pltpu.get_barrier_semaphore()
    for i in range(1, n_st):
        pl.semaphore_signal(
            barrier, inc=1, device_id={"st": lax.rem(me + i, n_st)}, device_id_type=MESH
        )
    for i in range(1, n_dom):
        pl.semaphore_signal(
            barrier, inc=1, device_id={"dom": lax.rem(dom + i, n_dom)}, device_id_type=MESH
        )

    lane = lax.broadcasted_iota(jnp.int32, (ROWS, LANES), 1)
    z_pos = lane % NZ

    for field in fields:
        field[pl.ds(0, DEGREE)] = jnp.zeros((DEGREE, ROWS, width), jnp.float32)
        field[pl.ds(planes + DEGREE, DEGREE)] = jnp.zeros((DEGREE, ROWS, width), jnp.float32)

    pl.semaphore_wait(barrier, n_st - 1 + n_dom - 1)

    def halo_copy(side, c):
        begin = planes - ROWS if side == 0 else 0
        target = jnp.clip(dom + 1 if side == 0 else dom - 1, 0, n_dom - 1)
        return pltpu.make_async_remote_copy(
            src_ref=orb.at[pl.ds(c * ROWS, ROWS), pl.ds(begin, ROWS)],
            dst_ref=halo.at[side, c],
            send_sem=halo_send.at[side, c],
            recv_sem=halo_recv.at[side, c],
            device_id={"dom": target},
            device_id_type=MESH,
        )

    def pot_halo_copy(side):
        begin = planes - ROWS if side == 0 else 0
        target = jnp.clip(dom + 1 if side == 0 else dom - 1, 0, n_dom - 1)
        return pltpu.make_async_remote_copy(
            src_ref=pot.at[pl.ds(begin, ROWS)],
            dst_ref=pot_halo.at[side],
            send_sem=ph_send.at[side],
            recv_sem=ph_recv.at[side],
            device_id={"dom": target},
            device_id_type=MESH,
        )

    has_next = dom < n_dom - 1
    has_prev = dom > 0
    sends_side = (has_next, has_prev)
    takes_side = (has_prev, has_next)

    for side in range(2):
        @pl.when(sends_side[side])
        def _():
            pot_halo_copy(side).start()
            for c in range(chunks):
                halo_copy(side, c).start()

    part = dom if parts > 1 else 0
    my_rows = rot.at[pl.ds(pl.multiple_of(part * part_rows, ROWS), part_rows)]

    def rot_copy(i, owner):
        return pltpu.make_async_remote_copy(
            src_ref=my_rows,
            dst_ref=rot_full.at[owner, part],
            send_sem=r_send.at[i],
            recv_sem=r_recv.at[owner],
            device_id={"st": lax.rem(me + i, n_st)},
            device_id_type=MESH,
        )

    for i in range(1, n_st):
        rot_copy(i, me).start()
    rot_own = pltpu.make_async_copy(my_rows, rot_full.at[me, part], r_own)
    rot_own.start()

    def set_alpha(source, source_row, q):
        row = 2.0 * (source.astype(jnp.float32) - (cheb_shift - 3.0))
        for i in range(ROWS):
            if source_row[0] <= i < source_row[1]:
                alpha[q + i - source_row[0]] = jnp.broadcast_to(row[i : i + 1], (8, width))

    pot_copy.wait()

    def alpha_rows(j, carry):
        set_alpha(pot_v[pl.ds(pl.multiple_of(j * ROWS, ROWS), ROWS)], (0, ROWS), DEGREE + j * ROWS)
        return carry

    lax.fori_loop(0, planes // ROWS, alpha_rows, 0)

    def turned(value):
        return jnp.swapaxes(value.astype(jnp.float32), 0, 1)

    def advance(k, q, c, b):
        source = fields[k - 1]
        values = [source[q, :, pl.ds(i * LANES, LANES)] for i in range(cols)]
        ups = [pltpu.roll(v, LANES - NZ, 1) for v in values]
        downs = [pltpu.roll(v, NZ, 1) for v in values]
        zero = jnp.zeros((ROWS, LANES), jnp.float32)
        for i in range(cols):
            at = pl.ds(i * LANES, LANES)
            v = values[i]
            upper_z = jnp.where(z_pos < NZ - 1, pltpu.roll(v, LANES - 1, 1), 0.0)
            lower_z = jnp.where(z_pos > 0, pltpu.roll(v, 1, 1), 0.0)
            upper_y = jnp.where(lane < LANES - NZ, ups[i], ups[i + 1] if i + 1 < cols else zero)
            lower_y = jnp.where(lane >= NZ, downs[i], downs[i - 1] if i else zero)
            beside = (source[q + 1, :, at] + source[q - 1, :, at]) + (upper_y + lower_y)
            beside = beside + (upper_z + lower_z)
            a8 = alpha[q, :, at]
            applied = jnp.concatenate([a8] * (ROWS // 8), axis=0) * v - beside
            if k == 1:
                result = applied * (0.5 / cheb_scale)
            else:
                result = applied * (1.0 / cheb_scale) - fields[k - 2][q, :, at]
            if k < DEGREE:
                fields[k][q, :, at] = result
            else:
                offset = (q - DEGREE - b * block) * width + i * LANES
                stage[c, b, :, pl.ds(pl.multiple_of(offset, LANES), LANES)] = result.astype(
                    jnp.bfloat16
                )

    def send_copy(c, b):
        return pltpu.make_async_remote_copy(
            src_ref=stage.at[c, b],
            dst_ref=gathered.at[pl.ds(pl.multiple_of(me * states + c * ROWS, ROWS), ROWS)],
            send_sem=send_sem.at[c, b],
            recv_sem=recv_sem.at[c, me],
            device_id={"st": b},
            device_id_type=MESH,
        )

    def own_copy(c):
        return pltpu.make_async_copy(
            stage.at[c, me],
            gathered.at[pl.ds(pl.multiple_of(me * states + c * ROWS, ROWS), ROWS)],
            own_sem.at[c],
        )

    up_first = (me < half).astype(jnp.int32)
    halo_blocks = -(-DEGREE // block)

    def chunk_body(c, carry):
        load(c).wait()

        def turn(j, inner):
            at_planes = pl.ds(pl.multiple_of(j * ROWS, ROWS), ROWS)
            for i in range(cols):
                at = pl.ds(i * LANES, LANES)
                value = raw[pl.ds(pl.multiple_of(c * ROWS, ROWS), ROWS), at_planes, at]
                y0[pl.ds(DEGREE + j * ROWS, ROWS), :, at] = turned(value)
            return inner

        lax.fori_loop(0, planes // ROWS, turn, 0)

        def step_body(step, inner):
            in_first = (step < half).astype(jnp.int32)
            j = jnp.where(step < half, step, step - half)
            up = in_first * up_first + (1 - in_first) * (1 - up_first)
            b = up * (half + j) + (1 - up) * (half - 1 - j)

            for side in range(2):
                @pl.when((j == half - halo_blocks) & (up == side) & takes_side[side])
                def _():
                    halo_copy(side, c).wait_recv()
                    begin = ROWS - DEGREE if side == 0 else 0
                    q = 0 if side == 0 else planes + DEGREE
                    for i in range(cols):
                        at = pl.ds(i * LANES, LANES)
                        y0[pl.ds(q, DEGREE), :, at] = turned(halo[side, c, :, :, at])[
                            begin : begin + DEGREE
                        ]

                    @pl.when(c == 0)
                    def _():
                        pot_halo_copy(side).wait_recv()
                        set_alpha(pot_halo[side], (begin, begin + DEGREE), q)

            is_start = (step == 0).astype(jnp.int32)
            for k in range(1, DEGREE + 1):
                reach = DEGREE - k
                low = b * block + DEGREE - reach + 2 * reach * up * (1 - is_start)
                high = b * block + block + DEGREE - reach + 2 * reach * jnp.maximum(up, is_start)
                low = jnp.maximum(low, jnp.where(has_prev, k, DEGREE))
                high = jnp.minimum(
                    high, jnp.where(has_next, planes + DEGREE + reach, planes + DEGREE)
                )

                def plane_body(q, nothing):
                    advance(k, q, c, b)
                    return nothing

                lax.fori_loop(low, high, plane_body, 0)

            @pl.when(b != me)
            def _():
                send_copy(c, b).start()

            @pl.when(b == me)
            def _():
                own_copy(c).start()

            return inner

        lax.fori_loop(0, n_st, step_body, 0)
        return carry

    lax.fori_loop(0, chunks, chunk_body, 0)

    for i in range(1, n_st):
        rot_copy(i, lax.rem(me + i, n_st)).wait_recv()
    rot_own.wait()
    if parts > 1:
        def spread_copy(i, owner):
            return pltpu.make_async_remote_copy(
                src_ref=rot_full.at[:, owner],
                dst_ref=rot_full.at[:, owner],
                send_sem=r2_send.at[i],
                recv_sem=r2_recv.at[owner],
                device_id={"dom": lax.rem(dom + i, n_dom)},
                device_id_type=MESH,
            )

        for i in range(1, n_dom):
            spread_copy(i, dom).start()
        for i in range(1, n_dom):
            spread_copy(i, dom).wait_send()
            spread_copy(i, lax.rem(dom + i, n_dom)).wait_recv()
    for i in range(1, n_st):
        rot_copy(i, me).wait_send()
    for side in range(2):
        @pl.when(sends_side[side])
        def _():
            pot_halo_copy(side).wait_send()
            for c in range(chunks):
                halo_copy(side, c).wait_send()

    def arrival(c, i):
        peer = lax.rem(me + i, n_st)
        return pltpu.make_async_remote_copy(
            src_ref=stage.at[c, peer],
            dst_ref=gathered.at[pl.ds(pl.multiple_of(peer * states + c * ROWS, ROWS), ROWS)],
            send_sem=send_sem.at[c, peer],
            recv_sem=recv_sem.at[c, peer],
            device_id={"st": peer},
            device_id_type=MESH,
        )

    def finish(c, carry):
        def finish_peer(i, inner):
            arrival(c, i).wait_send()
            arrival(c, i).wait_recv()
            return inner

        lax.fori_loop(1, n_st, finish_peer, 0)
        own_copy(c).wait()
        return carry

    lax.fori_loop(0, chunks, finish, 0)


def rotate_kernel(rot, states, out):
    out[...] = jnp.dot(rot[...], states[...], preferred_element_type=jnp.float32).astype(out.dtype)


def local(n_dom, n_st, orbitals, potential, rotation):
    states, planes, width = orbitals.shape
    total = rotation.shape[1]
    chunks = states // ROWS
    block = planes // n_st
    points = block * width
    parts = n_dom if states % (ROWS * n_dom) == 0 else 1
    field = pltpu.VMEM((planes + 2 * DEGREE, ROWS, width), jnp.float32)
    dma = pltpu.SemaphoreType.DMA
    anywhere = pl.BlockSpec(memory_space=pl.ANY)
    gathered, rot_full = pl.pallas_call(
        functools.partial(filter_kernel, n_dom, n_st, parts),
        out_shape=(
            jax.ShapeDtypeStruct((n_st * states, points), jnp.bfloat16),
            jax.ShapeDtypeStruct((n_st, parts, states // parts, total), jnp.bfloat16),
        ),
        in_specs=[anywhere] * 3,
        out_specs=(anywhere, anywhere),
        scratch_shapes=[
            pltpu.VMEM((states, planes, width), jnp.bfloat16),
            pltpu.VMEM((2, chunks, ROWS, ROWS, width), jnp.bfloat16),
            pltpu.VMEM((planes, width), jnp.bfloat16),
            pltpu.VMEM((2, ROWS, width), jnp.bfloat16),
            pltpu.VMEM((planes + 2 * DEGREE, 8, width), jnp.float32),
            field, field, field, field,
            pltpu.VMEM((chunks, n_st, ROWS, points), jnp.bfloat16),
            dma((chunks,)), dma,
            dma((2, chunks)), dma((2, chunks)), dma((2,)), dma((2,)),
            dma((chunks, n_st)), dma((chunks, n_st)), dma((chunks,)),
            dma((n_st,)), dma((n_st,)), dma,
            dma((n_dom,)), dma((n_dom,)),
        ],
        compiler_params=pltpu.CompilerParams(
            collective_id=0, has_side_effects=True, vmem_limit_bytes=56 * 1024 * 1024
        ),
        cost_estimate=pl.CostEstimate(
            flops=13 * DEGREE * states * planes * width,
            bytes_accessed=4 * states * planes * width,
            transcendentals=0,
        ),
        name="filter_exchange",
    )(orbitals, potential, rotation)
    rot_all = rot_full.reshape(n_st * states, total)
    return pl.pallas_call(
        rotate_kernel,
        out_shape=jax.ShapeDtypeStruct((n_st * states, points), jnp.bfloat16),
        grid=(points // width,),
        in_specs=[
            pl.BlockSpec((n_st * states, total), lambda i: (0, 0)),
            pl.BlockSpec((n_st * states, width), lambda i: (0, i)),
        ],
        out_specs=pl.BlockSpec((n_st * states, width), lambda i: (0, i)),
        compiler_params=pltpu.CompilerParams(vmem_limit_bytes=32 * 1024 * 1024),
        cost_estimate=pl.CostEstimate(
            flops=2 * n_st * states * total * points,
            bytes_accessed=4 * n_st * states * points,
            transcendentals=0,
        ),
        name="rotate",
    )(rot_all, gathered)


def solution(mesh):
    return jax.shard_map(
        functools.partial(local, mesh.shape["dom"], mesh.shape["st"]),
        mesh=mesh,
        in_specs=(P("st", "dom", None), P("dom", None), P("st", None)),
        out_specs=P(None, ("dom", "st")),
        check_vma=False,
    )
```

```python
import functools

import jax
import jax.numpy as jnp
from jax import lax
from jax.experimental import pallas as pl
from jax.experimental.pallas import tpu as pltpu
from jax.sharding import PartitionSpec as P

DEGREE = 4
NZ = 32
LANES = 128
ROWS = 16
MESH = pl.DeviceIdType.MESH

cheb_shift = 3.75
cheb_scale = 3.25


def filter_kernel(
    n_dom, n_st, parts,
    orb, pot, rot,
    gathered, rot_full,
    raw, halo, pot_v, pot_halo, alpha, y0, y1, y2, y3, stage,
    load_sem, pot_sem, halo_send, halo_recv, ph_send, ph_recv,
    send_sem, recv_sem, own_sem, r_send, r_recv, r_own, r2_send, r2_recv,
):
    dom = lax.axis_index("dom")
    me = lax.axis_index("st")
    states, planes, width = orb.shape
    chunks = states // ROWS
    block = planes // n_st
    half = n_st // 2
    cols = width // LANES
    part_rows = states // parts
    fields = (y0, y1, y2, y3)

    def load(c):
        return pltpu.make_async_copy(
            orb.at[pl.ds(c * ROWS, ROWS)], raw.at[pl.ds(c * ROWS, ROWS)], load_sem.at[c]
        )

    for c in range(chunks):
        load(c).start()
    pot_copy = pltpu.make_async_copy(pot, pot_v, pot_sem)
    pot_copy.start()

    barrier = pltpu.get_barrier_semaphore()
    for i in range(1, n_st):
        pl.semaphore_signal(
            barrier, inc=1, device_id={"st": lax.rem(me + i, n_st)}, device_id_type=MESH
        )
    for i in range(1, n_dom):
        pl.semaphore_signal(
            barrier, inc=1, device_id={"dom": lax.rem(dom + i, n_dom)}, device_id_type=MESH
        )

    lane = lax.broadcasted_iota(jnp.int32, (ROWS, LANES), 1)
    z_pos = lane % NZ

    for field in fields:
        field[pl.ds(0, DEGREE)] = jnp.zeros((DEGREE, ROWS, width), jnp.float32)
        field[pl.ds(planes + DEGREE, DEGREE)] = jnp.zeros((DEGREE, ROWS, width), jnp.float32)

    pl.semaphore_wait(barrier, n_st - 1 + n_dom - 1)

    def halo_copy(side, c):
        begin = planes - ROWS if side == 0 else 0
        target = jnp.clip(dom + 1 if side == 0 else dom - 1, 0, n_dom - 1)
        return pltpu.make_async_remote_copy(
            src_ref=orb.at[pl.ds(c * ROWS, ROWS), pl.ds(begin, ROWS)],
            dst_ref=halo.at[side, c],
            send_sem=halo_send.at[side, c],
            recv_sem=halo_recv.at[side, c],
            device_id={"dom": target},
            device_id_type=MESH,
        )

    def pot_halo_copy(side):
        begin = planes - ROWS if side == 0 else 0
        target = jnp.clip(dom + 1 if side == 0 else dom - 1, 0, n_dom - 1)
        return pltpu.make_async_remote_copy(
            src_ref=pot.at[pl.ds(begin, ROWS)],
            dst_ref=pot_halo.at[side],
            send_sem=ph_send.at[side],
            recv_sem=ph_recv.at[side],
            device_id={"dom": target},
            device_id_type=MESH,
        )

    has_next = dom < n_dom - 1
    has_prev = dom > 0
    sends_side = (has_next, has_prev)
    takes_side = (has_prev, has_next)

    for side in range(2):
        @pl.when(sends_side[side])
        def _():
            pot_halo_copy(side).start()
            for c in range(chunks):
                halo_copy(side, c).start()

    part = dom if parts > 1 else 0
    my_rows = rot.at[pl.ds(pl.multiple_of(part * part_rows, ROWS), part_rows)]

    def rot_copy(i, owner):
        return pltpu.make_async_remote_copy(
            src_ref=my_rows,
            dst_ref=rot_full.at[owner, part],
            send_sem=r_send.at[i],
            recv_sem=r_recv.at[owner],
            device_id={"st": lax.rem(me + i, n_st)},
            device_id_type=MESH,
        )

    for i in range(1, n_st):
        rot_copy(i, me).start()
    rot_own = pltpu.make_async_copy(my_rows, rot_full.at[me, part], r_own)
    rot_own.start()

    def set_alpha(source, source_row, q):
        row = 2.0 * (source.astype(jnp.float32) - (cheb_shift - 3.0))
        for i in range(ROWS):
            if source_row[0] <= i < source_row[1]:
                alpha[q + i - source_row[0]] = jnp.broadcast_to(row[i : i + 1], (8, width))

    pot_copy.wait()

    def alpha_rows(j, carry):
        set_alpha(pot_v[pl.ds(pl.multiple_of(j * ROWS, ROWS), ROWS)], (0, ROWS), DEGREE + j * ROWS)
        return carry

    lax.fori_loop(0, planes // ROWS, alpha_rows, 0)

    def turned(value):
        return jnp.swapaxes(value.astype(jnp.float32), 0, 1)

    def advance(k, q, c, b):
        source = fields[k - 1]
        values = [source[q, :, pl.ds(i * LANES, LANES)] for i in range(cols)]
        ups = [pltpu.roll(v, LANES - NZ, 1) for v in values]
        downs = [pltpu.roll(v, NZ, 1) for v in values]
        zero = jnp.zeros((ROWS, LANES), jnp.float32)
        for i in range(cols):
            at = pl.ds(i * LANES, LANES)
            v = values[i]
            upper_z = jnp.where(z_pos < NZ - 1, pltpu.roll(v, LANES - 1, 1), 0.0)
            lower_z = jnp.where(z_pos > 0, pltpu.roll(v, 1, 1), 0.0)
            upper_y = jnp.where(lane < LANES - NZ, ups[i], ups[i + 1] if i + 1 < cols else zero)
            lower_y = jnp.where(lane >= NZ, downs[i], downs[i - 1] if i else zero)
            beside = (source[q + 1, :, at] + source[q - 1, :, at]) + (upper_y + lower_y)
            beside = beside + (upper_z + lower_z)
            a8 = alpha[q, :, at]
            applied = jnp.concatenate([a8] * (ROWS // 8), axis=0) * v - beside
            if k == 1:
                result = applied * (0.5 / cheb_scale)
            else:
                result = applied * (1.0 / cheb_scale) - fields[k - 2][q, :, at]
            if k < DEGREE:
                fields[k][q, :, at] = result
            else:
                offset = (q - DEGREE - b * block) * width + i * LANES
                stage[c, b, :, pl.ds(pl.multiple_of(offset, LANES), LANES)] = result.astype(
                    jnp.bfloat16
                )

    def send_copy(c, b):
        return pltpu.make_async_remote_copy(
            src_ref=stage.at[c, b],
            dst_ref=gathered.at[pl.ds(pl.multiple_of(me * states + c * ROWS, ROWS), ROWS)],
            send_sem=send_sem.at[c, b],
            recv_sem=recv_sem.at[c, me],
            device_id={"st": b},
            device_id_type=MESH,
        )

    def own_copy(c):
        return pltpu.make_async_copy(
            stage.at[c, me],
            gathered.at[pl.ds(pl.multiple_of(me * states + c * ROWS, ROWS), ROWS)],
            own_sem.at[c],
        )

    up_first = me < half
    odd = lax.rem(me, 2) if half > 1 else 0
    even = 1 - odd if half > 1 else 0
    pivot = jnp.where(up_first, half + odd, half - 1 - even)
    halo_blocks = -(-DEGREE // block)
    last = chunks - 1

    def block_at(step):
        upper = jnp.where(step < n_st - pivot, pivot + step, n_st - 1 - step)
        lower = jnp.where(step <= pivot, pivot - step, step)
        return jnp.where(up_first, upper, lower)

    def issue(c, b):
        @pl.when(b != me)
        def _():
            send_copy(c, b).start()

        @pl.when(b == me)
        def _():
            own_copy(c).start()

    def chunk_body(c, carry):
        load(c).wait()

        def turn(j, inner):
            at_planes = pl.ds(pl.multiple_of(j * ROWS, ROWS), ROWS)
            for i in range(cols):
                at = pl.ds(i * LANES, LANES)
                value = raw[pl.ds(pl.multiple_of(c * ROWS, ROWS), ROWS), at_planes, at]
                y0[pl.ds(DEGREE + j * ROWS, ROWS), :, at] = turned(value)
            return inner

        begin_row = jnp.maximum(pivot * block - DEGREE, 0) // ROWS
        end_row = jnp.minimum((pivot * block + block + DEGREE - 1) // ROWS + 1, planes // ROWS)

        def step_body(step, inner):
            b = block_at(step)
            up = jnp.where(
                up_first, (step < n_st - pivot).astype(jnp.int32), (step > pivot).astype(jnp.int32)
            )
            is_start = (step == 0).astype(jnp.int32)

            @pl.when(step == 0)
            def _():
                lax.fori_loop(begin_row, end_row, turn, 0)

            @pl.when(step == 1)
            def _():
                lax.fori_loop(0, begin_row, turn, 0)
                lax.fori_loop(end_row, planes // ROWS, turn, 0)

            for side in range(2):
                needed = n_st - halo_blocks if side else halo_blocks - 1

                @pl.when((b == needed) & (up == side) & takes_side[side])
                def _():
                    halo_copy(side, c).wait_recv()
                    begin = ROWS - DEGREE if side == 0 else 0
                    q = 0 if side == 0 else planes + DEGREE
                    for i in range(cols):
                        at = pl.ds(i * LANES, LANES)
                        y0[pl.ds(q, DEGREE), :, at] = turned(halo[side, c, :, :, at])[
                            begin : begin + DEGREE
                        ]

                    @pl.when(c == 0)
                    def _():
                        pot_halo_copy(side).wait_recv()
                        set_alpha(pot_halo[side], (begin, begin + DEGREE), q)

            for k in range(1, DEGREE + 1):
                reach = DEGREE - k
                low = b * block + DEGREE - reach + 2 * reach * up * (1 - is_start)
                high = b * block + block + DEGREE - reach + 2 * reach * jnp.maximum(up, is_start)
                low = jnp.maximum(low, jnp.where(has_prev, k, DEGREE))
                high = jnp.minimum(
                    high, jnp.where(has_next, planes + DEGREE + reach, planes + DEGREE)
                )

                def plane_body(q, nothing):
                    advance(k, q, c, b)
                    return nothing

                lax.fori_loop(low, high, plane_body, 0)

            if chunks == 1:
                issue(c, b)
            else:
                @pl.when((step < half) & (c > 0))
                def _():
                    issue(c - 1, block_at(step + half))

                @pl.when((step < half) & (c < last))
                def _():
                    issue(c, b)

                @pl.when((step >= half) & (c == last))
                def _():
                    issue(c, b)
                    issue(c, block_at(step - half))

            return inner

        lax.fori_loop(0, n_st, step_body, 0)
        return carry

    lax.fori_loop(0, chunks, chunk_body, 0)

    for i in range(1, n_st):
        rot_copy(i, lax.rem(me + i, n_st)).wait_recv()
    rot_own.wait()
    if parts > 1:
        def spread_copy(i, owner):
            return pltpu.make_async_remote_copy(
                src_ref=rot_full.at[:, owner],
                dst_ref=rot_full.at[:, owner],
                send_sem=r2_send.at[i],
                recv_sem=r2_recv.at[owner],
                device_id={"dom": lax.rem(dom + i, n_dom)},
                device_id_type=MESH,
            )

        for i in range(1, n_dom):
            spread_copy(i, dom).start()
        for i in range(1, n_dom):
            spread_copy(i, dom).wait_send()
            spread_copy(i, lax.rem(dom + i, n_dom)).wait_recv()
    for i in range(1, n_st):
        rot_copy(i, me).wait_send()
    for side in range(2):
        @pl.when(sends_side[side])
        def _():
            pot_halo_copy(side).wait_send()
            for c in range(chunks):
                halo_copy(side, c).wait_send()

    def arrival(c, i):
        peer = lax.rem(me + i, n_st)
        return pltpu.make_async_remote_copy(
            src_ref=stage.at[c, peer],
            dst_ref=gathered.at[pl.ds(pl.multiple_of(peer * states + c * ROWS, ROWS), ROWS)],
            send_sem=send_sem.at[c, peer],
            recv_sem=recv_sem.at[c, peer],
            device_id={"st": peer},
            device_id_type=MESH,
        )

    def finish(c, carry):
        def finish_peer(i, inner):
            arrival(c, i).wait_send()
            arrival(c, i).wait_recv()
            return inner

        lax.fori_loop(1, n_st, finish_peer, 0)
        own_copy(c).wait()
        return carry

    lax.fori_loop(0, chunks, finish, 0)


def rotate_kernel(rot, states, out):
    out[...] = jnp.dot(rot[...], states[...], preferred_element_type=jnp.float32).astype(out.dtype)


def local(n_dom, n_st, orbitals, potential, rotation):
    states, planes, width = orbitals.shape
    total = rotation.shape[1]
    chunks = states // ROWS
    block = planes // n_st
    points = block * width
    parts = n_dom if states % (ROWS * n_dom) == 0 else 1
    field = pltpu.VMEM((planes + 2 * DEGREE, ROWS, width), jnp.float32)
    dma = pltpu.SemaphoreType.DMA
    anywhere = pl.BlockSpec(memory_space=pl.ANY)
    gathered, rot_full = pl.pallas_call(
        functools.partial(filter_kernel, n_dom, n_st, parts),
        out_shape=(
            jax.ShapeDtypeStruct((n_st * states, points), jnp.bfloat16),
            jax.ShapeDtypeStruct((n_st, parts, states // parts, total), jnp.bfloat16),
        ),
        in_specs=[anywhere] * 3,
        out_specs=(anywhere, anywhere),
        scratch_shapes=[
            pltpu.VMEM((states, planes, width), jnp.bfloat16),
            pltpu.VMEM((2, chunks, ROWS, ROWS, width), jnp.bfloat16),
            pltpu.VMEM((planes, width), jnp.bfloat16),
            pltpu.VMEM((2, ROWS, width), jnp.bfloat16),
            pltpu.VMEM((planes + 2 * DEGREE, 8, width), jnp.float32),
            field, field, field, field,
            pltpu.VMEM((chunks, n_st, ROWS, points), jnp.bfloat16),
            dma((chunks,)), dma,
            dma((2, chunks)), dma((2, chunks)), dma((2,)), dma((2,)),
            dma((chunks, n_st)), dma((chunks, n_st)), dma((chunks,)),
            dma((n_st,)), dma((n_st,)), dma,
            dma((n_dom,)), dma((n_dom,)),
        ],
        compiler_params=pltpu.CompilerParams(
            collective_id=0, has_side_effects=True, vmem_limit_bytes=56 * 1024 * 1024
        ),
        cost_estimate=pl.CostEstimate(
            flops=13 * DEGREE * states * planes * width,
            bytes_accessed=4 * states * planes * width,
            transcendentals=0,
        ),
        name="filter_exchange",
    )(orbitals, potential, rotation)
    rot_all = rot_full.reshape(n_st * states, total)
    return pl.pallas_call(
        rotate_kernel,
        out_shape=jax.ShapeDtypeStruct((n_st * states, points), jnp.bfloat16),
        grid=(points // width,),
        in_specs=[
            pl.BlockSpec((n_st * states, total), lambda i: (0, 0)),
            pl.BlockSpec((n_st * states, width), lambda i: (0, i)),
        ],
        out_specs=pl.BlockSpec((n_st * states, width), lambda i: (0, i)),
        compiler_params=pltpu.CompilerParams(vmem_limit_bytes=60 * 1024 * 1024),
        cost_estimate=pl.CostEstimate(
            flops=2 * n_st * states * total * points,
            bytes_accessed=4 * n_st * states * points,
            transcendentals=0,
        ),
        name="rotate",
    )(rot_all, gathered)


def solution(mesh):
    return jax.shard_map(
        functools.partial(local, mesh.shape["dom"], mesh.shape["st"]),
        mesh=mesh,
        in_specs=(P("st", "dom", None), P("dom", None), P("st", None)),
        out_specs=P(None, ("dom", "st")),
        check_vma=False,
    )
```

```python
import functools

import jax
import jax.numpy as jnp
from jax import lax
from jax.experimental import pallas as pl
from jax.experimental.pallas import tpu as pltpu
from jax.sharding import PartitionSpec as P

DEGREE = 4
NZ = 32
LANES = 128
ROWS = 16
MESH = pl.DeviceIdType.MESH

cheb_shift = 3.75
cheb_scale = 3.25


def filter_kernel(
    n_dom, n_st, parts,
    orb, pot, rot,
    rotated1, gathered2, rot_full,
    raw, halo, pot_v, pot_halo, alpha, y0, y1, y2, y3, stage1, stage2, gathered1, rot_v, turn_out,
    load_sem, pot_sem, halo_send, halo_recv, ph_send, ph_recv,
    send_sem, recv_sem, own_sem, r_send, r_recv, r_own, r2_send, r2_recv, out_sem,
):
    dom = lax.axis_index("dom")
    me = lax.axis_index("st")
    states, planes, width = orb.shape
    chunks = states // ROWS
    block = planes // n_st
    late = gathered2.shape[1] // width
    early = block - late
    half = n_st // 2
    cols = width // LANES
    part_rows = states // parts
    fields = (y0, y1, y2, y3)
    stages = (stage1, stage2)
    gathers = (gathered1, gathered2)

    def load(c):
        return pltpu.make_async_copy(
            orb.at[pl.ds(c * ROWS, ROWS)], raw.at[pl.ds(c * ROWS, ROWS)], load_sem.at[c]
        )

    for c in range(chunks):
        load(c).start()
    pot_copy = pltpu.make_async_copy(pot, pot_v, pot_sem)
    pot_copy.start()

    barrier = pltpu.get_barrier_semaphore()
    for i in range(1, n_st):
        pl.semaphore_signal(
            barrier, inc=1, device_id={"st": lax.rem(me + i, n_st)}, device_id_type=MESH
        )
    for i in range(1, n_dom):
        pl.semaphore_signal(
            barrier, inc=1, device_id={"dom": lax.rem(dom + i, n_dom)}, device_id_type=MESH
        )

    lane = lax.broadcasted_iota(jnp.int32, (ROWS, LANES), 1)
    z_pos = lane % NZ

    for field in fields:
        field[pl.ds(0, DEGREE)] = jnp.zeros((DEGREE, ROWS, width), jnp.float32)
        field[pl.ds(planes + DEGREE, DEGREE)] = jnp.zeros((DEGREE, ROWS, width), jnp.float32)

    pl.semaphore_wait(barrier, n_st - 1 + n_dom - 1)

    def halo_copy(side, c):
        begin = planes - ROWS if side == 0 else 0
        target = jnp.clip(dom + 1 if side == 0 else dom - 1, 0, n_dom - 1)
        return pltpu.make_async_remote_copy(
            src_ref=orb.at[pl.ds(c * ROWS, ROWS), pl.ds(begin, ROWS)],
            dst_ref=halo.at[side, c],
            send_sem=halo_send.at[side, c],
            recv_sem=halo_recv.at[side, c],
            device_id={"dom": target},
            device_id_type=MESH,
        )

    def pot_halo_copy(side):
        begin = planes - ROWS if side == 0 else 0
        target = jnp.clip(dom + 1 if side == 0 else dom - 1, 0, n_dom - 1)
        return pltpu.make_async_remote_copy(
            src_ref=pot.at[pl.ds(begin, ROWS)],
            dst_ref=pot_halo.at[side],
            send_sem=ph_send.at[side],
            recv_sem=ph_recv.at[side],
            device_id={"dom": target},
            device_id_type=MESH,
        )

    has_next = dom < n_dom - 1
    has_prev = dom > 0
    sends_side = (has_next, has_prev)
    takes_side = (has_prev, has_next)

    for side in range(2):
        @pl.when(sends_side[side])
        def _():
            pot_halo_copy(side).start()
            for c in range(chunks):
                halo_copy(side, c).start()

    part = dom if parts > 1 else 0
    my_rows = rot.at[pl.ds(pl.multiple_of(part * part_rows, ROWS), part_rows)]

    def rot_copy(i, owner):
        return pltpu.make_async_remote_copy(
            src_ref=my_rows,
            dst_ref=rot_full.at[owner, part],
            send_sem=r_send.at[i],
            recv_sem=r_recv.at[owner],
            device_id={"st": lax.rem(me + i, n_st)},
            device_id_type=MESH,
        )

    for i in range(1, n_st):
        rot_copy(i, me).start()
    rot_own = pltpu.make_async_copy(my_rows, rot_full.at[me, part], r_own)
    rot_own.start()

    def set_alpha(source, source_row, q):
        row = 2.0 * (source.astype(jnp.float32) - (cheb_shift - 3.0))
        for i in range(ROWS):
            if source_row[0] <= i < source_row[1]:
                alpha[q + i - source_row[0]] = jnp.broadcast_to(row[i : i + 1], (8, width))

    pot_copy.wait()

    def alpha_rows(j, carry):
        set_alpha(pot_v[pl.ds(pl.multiple_of(j * ROWS, ROWS), ROWS)], (0, ROWS), DEGREE + j * ROWS)
        return carry

    lax.fori_loop(0, planes // ROWS, alpha_rows, 0)

    def turned(value):
        return jnp.swapaxes(value.astype(jnp.float32), 0, 1)

    def advance(k, q, c, b, piece):
        source = fields[k - 1]
        values = [source[q, :, pl.ds(i * LANES, LANES)] for i in range(cols)]
        ups = [pltpu.roll(v, LANES - NZ, 1) for v in values]
        downs = [pltpu.roll(v, NZ, 1) for v in values]
        zero = jnp.zeros((ROWS, LANES), jnp.float32)
        for i in range(cols):
            at = pl.ds(i * LANES, LANES)
            v = values[i]
            upper_z = jnp.where(z_pos < NZ - 1, pltpu.roll(v, LANES - 1, 1), 0.0)
            lower_z = jnp.where(z_pos > 0, pltpu.roll(v, 1, 1), 0.0)
            upper_y = jnp.where(lane < LANES - NZ, ups[i], ups[i + 1] if i + 1 < cols else zero)
            lower_y = jnp.where(lane >= NZ, downs[i], downs[i - 1] if i else zero)
            beside = (source[q + 1, :, at] + source[q - 1, :, at]) + (upper_y + lower_y)
            beside = beside + (upper_z + lower_z)
            a8 = alpha[q, :, at]
            applied = jnp.concatenate([a8] * (ROWS // 8), axis=0) * v - beside
            if k == 1:
                result = applied * (0.5 / cheb_scale)
            else:
                result = applied * (1.0 / cheb_scale) - fields[k - 2][q, :, at]
            if k < DEGREE:
                fields[k][q, :, at] = result
            else:
                offset = (q - DEGREE - b * block - piece * early) * width + i * LANES
                stages[piece][c, b, :, pl.ds(pl.multiple_of(offset, LANES), LANES)] = result.astype(
                    jnp.bfloat16
                )

    def rows_of(owner, c):
        return pl.ds(pl.multiple_of(owner * states + c * ROWS, ROWS), ROWS)

    def send_copy(piece, c, b):
        return pltpu.make_async_remote_copy(
            src_ref=stages[piece].at[c, b],
            dst_ref=gathers[piece].at[rows_of(me, c)],
            send_sem=send_sem.at[piece, c, b],
            recv_sem=recv_sem.at[piece, c, me],
            device_id={"st": b},
            device_id_type=MESH,
        )

    def own_copy(piece, c):
        return pltpu.make_async_copy(
            stages[piece].at[c, me], gathers[piece].at[rows_of(me, c)], own_sem.at[piece, c]
        )

    up_first = me < half
    odd = lax.rem(me, 2) if half > 1 else 0
    even = 1 - odd if half > 1 else 0
    pivot = jnp.where(up_first, half + odd, half - 1 - even)
    halo_blocks = -(-DEGREE // block)
    last = chunks - 1

    def block_at(step):
        upper = jnp.where(step < n_st - pivot, pivot + step, n_st - 1 - step)
        lower = jnp.where(step <= pivot, pivot - step, step)
        return jnp.where(up_first, upper, lower)

    def issue(piece, c, b):
        @pl.when(b != me)
        def _():
            send_copy(piece, c, b).start()

        @pl.when(b == me)
        def _():
            own_copy(piece, c).start()

    def chunk_body(c, carry):
        load(c).wait()

        def turn(j, inner):
            at_planes = pl.ds(pl.multiple_of(j * ROWS, ROWS), ROWS)
            for i in range(cols):
                at = pl.ds(i * LANES, LANES)
                value = raw[pl.ds(pl.multiple_of(c * ROWS, ROWS), ROWS), at_planes, at]
                y0[pl.ds(DEGREE + j * ROWS, ROWS), :, at] = turned(value)
            return inner

        begin_row = jnp.maximum(pivot * block - DEGREE, 0) // ROWS
        end_row = jnp.minimum((pivot * block + block + DEGREE - 1) // ROWS + 1, planes // ROWS)

        def step_body(step, inner):
            b = block_at(step)
            up = jnp.where(
                up_first, (step < n_st - pivot).astype(jnp.int32), (step > pivot).astype(jnp.int32)
            )
            is_start = (step == 0).astype(jnp.int32)

            @pl.when(step == 0)
            def _():
                lax.fori_loop(begin_row, end_row, turn, 0)

            @pl.when(step == 1)
            def _():
                lax.fori_loop(0, begin_row, turn, 0)
                lax.fori_loop(end_row, planes // ROWS, turn, 0)

            for side in range(2):
                needed = n_st - halo_blocks if side else halo_blocks - 1

                @pl.when((b == needed) & (up == side) & takes_side[side])
                def _():
                    halo_copy(side, c).wait_recv()
                    begin = ROWS - DEGREE if side == 0 else 0
                    q = 0 if side == 0 else planes + DEGREE
                    for i in range(cols):
                        at = pl.ds(i * LANES, LANES)
                        y0[pl.ds(q, DEGREE), :, at] = turned(halo[side, c, :, :, at])[
                            begin : begin + DEGREE
                        ]

                    @pl.when(c == 0)
                    def _():
                        pot_halo_copy(side).wait_recv()
                        set_alpha(pot_halo[side], (begin, begin + DEGREE), q)

            for k in range(1, DEGREE + 1):
                reach = DEGREE - k
                low = b * block + DEGREE - reach + 2 * reach * up * (1 - is_start)
                high = b * block + block + DEGREE - reach + 2 * reach * jnp.maximum(up, is_start)
                low = jnp.maximum(low, jnp.where(has_prev, k, DEGREE))
                high = jnp.minimum(
                    high, jnp.where(has_next, planes + DEGREE + reach, planes + DEGREE)
                )

                def plane_body(piece, q, nothing):
                    advance(k, q, c, b, piece)
                    return nothing

                cut = b * block + DEGREE + early if k == DEGREE else high
                lax.fori_loop(low, cut, functools.partial(plane_body, 0), 0)
                if k == DEGREE:
                    lax.fori_loop(cut, high, functools.partial(plane_body, 1), 0)

            if chunks == 1:
                issue(0, c, b)
            else:
                @pl.when((step < half) & (c > 0))
                def _():
                    issue(0, c - 1, block_at(step + half))

                @pl.when((step < half) & (c < last))
                def _():
                    issue(0, c, b)

                @pl.when((step >= half) & (c == last))
                def _():
                    issue(0, c, b)
                    issue(0, c, block_at(step - half))

            return inner

        lax.fori_loop(0, n_st, step_body, 0)
        return carry

    lax.fori_loop(0, chunks, chunk_body, 0)

    def late_body(t, carry):
        c, j = t // half, lax.rem(t, half)
        issue(1, c, block_at(j + half))
        issue(1, c, block_at(j))
        return carry

    lax.fori_loop(0, chunks * half, late_body, 0)

    for i in range(1, n_st):
        rot_copy(i, lax.rem(me + i, n_st)).wait_recv()
    rot_own.wait()
    if parts > 1:
        def spread_copy(i, owner):
            return pltpu.make_async_remote_copy(
                src_ref=rot_full.at[:, owner],
                dst_ref=rot_full.at[:, owner],
                send_sem=r2_send.at[i],
                recv_sem=r2_recv.at[owner],
                device_id={"dom": lax.rem(dom + i, n_dom)},
                device_id_type=MESH,
            )

        for i in range(1, n_dom):
            spread_copy(i, dom).start()
        for i in range(1, n_dom):
            spread_copy(i, dom).wait_send()
            spread_copy(i, lax.rem(dom + i, n_dom)).wait_recv()
    for i in range(1, n_st):
        rot_copy(i, me).wait_send()
    for side in range(2):
        @pl.when(sends_side[side])
        def _():
            pot_halo_copy(side).wait_send()
            for c in range(chunks):
                halo_copy(side, c).wait_send()

    rot_load = pltpu.make_async_copy(rot_full, rot_v, r_own)
    rot_load.start()
    rot_load.wait()

    def arrival(piece, c, i):
        peer = lax.rem(me + i, n_st)
        return pltpu.make_async_remote_copy(
            src_ref=stages[piece].at[c, peer],
            dst_ref=gathers[piece].at[rows_of(peer, c)],
            send_sem=send_sem.at[piece, c, peer],
            recv_sem=recv_sem.at[piece, c, peer],
            device_id={"st": peer},
            device_id_type=MESH,
        )

    def finish(piece, c, carry):
        def finish_peer(i, inner):
            arrival(piece, c, i).wait_send()
            arrival(piece, c, i).wait_recv()
            return inner

        lax.fori_loop(1, n_st, finish_peer, 0)
        own_copy(piece, c).wait()
        return carry

    lax.fori_loop(0, chunks, functools.partial(finish, 0), 0)

    def columns(tile):
        return pl.ds(pl.multiple_of(tile * width, width), width)

    def out_copy(slot, tile):
        return pltpu.make_async_copy(
            turn_out.at[slot], rotated1.at[:, columns(tile)], out_sem.at[slot]
        )

    def rotate_tile(tile, carry):
        slot = lax.rem(tile, 2)

        @pl.when(tile >= 2)
        def _():
            out_copy(slot, tile - 2).wait()

        rows = n_st * states
        turn_out[slot] = jnp.dot(
            rot_v[...].reshape(rows, rows),
            gathered1[:, columns(tile)],
            preferred_element_type=jnp.float32,
        ).astype(jnp.bfloat16)
        out_copy(slot, tile).start()
        return carry

    lax.fori_loop(0, early, rotate_tile, 0)
    for tile in range(max(early - 2, 0), early):
        out_copy(tile % 2, tile).wait()

    lax.fori_loop(0, chunks, functools.partial(finish, 1), 0)


def rotate_kernel(rot, gathered, rotated1, out, rot_v, held, result, in_sem, copy_sem, out_sem):
    total, points = gathered.shape
    tiles = held.shape[0]
    width = points // tiles
    done = rotated1.shape[1]
    pieces = copy_sem.shape[0]
    loads = [pltpu.make_async_copy(rot, rot_v, in_sem.at[tiles])]
    for t in range(tiles):
        loads.append(
            pltpu.make_async_copy(
                gathered.at[:, pl.ds(t * width, width)], held.at[t], in_sem.at[t]
            )
        )
    copies = []
    for i in range(pieces):
        rows = pl.ds(i * (total // pieces), total // pieces)
        copies.append(
            pltpu.make_async_copy(rotated1.at[rows], out.at[rows, pl.ds(0, done)], copy_sem.at[i])
        )
    for copy in loads + copies:
        copy.start()
    loads[0].wait()
    stores = []
    for t in range(tiles):
        loads[t + 1].wait()
        result[t] = jnp.dot(
            rot_v[...], held[t], preferred_element_type=jnp.float32
        ).astype(out.dtype)
        store = pltpu.make_async_copy(
            result.at[t], out.at[:, pl.ds(done + t * width, width)], out_sem.at[t]
        )
        store.start()
        stores.append(store)
    for copy in copies + stores:
        copy.wait()


def local(n_dom, n_st, orbitals, potential, rotation):
    states, planes, width = orbitals.shape
    total = rotation.shape[1]
    chunks = states // ROWS
    block = planes // n_st
    late = max(block // 4, 1)
    points = block * width
    early_points = (block - late) * width
    late_points = late * width
    parts = n_dom if states % (ROWS * n_dom) == 0 else 1
    field = pltpu.VMEM((planes + 2 * DEGREE, ROWS, width), jnp.float32)
    dma = pltpu.SemaphoreType.DMA
    anywhere = pl.BlockSpec(memory_space=pl.ANY)
    rotated1, gathered2, rot_full = pl.pallas_call(
        functools.partial(filter_kernel, n_dom, n_st, parts),
        out_shape=(
            jax.ShapeDtypeStruct((n_st * states, early_points), jnp.bfloat16),
            jax.ShapeDtypeStruct((n_st * states, late_points), jnp.bfloat16),
            jax.ShapeDtypeStruct((n_st, parts, states // parts, total), jnp.bfloat16),
        ),
        in_specs=[anywhere] * 3,
        out_specs=(anywhere,) * 3,
        scratch_shapes=[
            pltpu.VMEM((states, planes, width), jnp.bfloat16),
            pltpu.VMEM((2, chunks, ROWS, ROWS, width), jnp.bfloat16),
            pltpu.VMEM((planes, width), jnp.bfloat16),
            pltpu.VMEM((2, ROWS, width), jnp.bfloat16),
            pltpu.VMEM((planes + 2 * DEGREE, 8, width), jnp.float32),
            field, field, field, field,
            pltpu.VMEM((chunks, n_st, ROWS, early_points), jnp.bfloat16),
            pltpu.VMEM((chunks, n_st, ROWS, late_points), jnp.bfloat16),
            pltpu.VMEM((n_st * states, early_points), jnp.bfloat16),
            pltpu.VMEM((n_st, parts, states // parts, total), jnp.bfloat16),
            pltpu.VMEM((2, n_st * states, width), jnp.bfloat16),
            dma((chunks,)), dma,
            dma((2, chunks)), dma((2, chunks)), dma((2,)), dma((2,)),
            dma((2, chunks, n_st)), dma((2, chunks, n_st)), dma((2, chunks)),
            dma((n_st,)), dma((n_st,)), dma,
            dma((n_dom,)), dma((n_dom,)), dma((2,)),
        ],
        compiler_params=pltpu.CompilerParams(
            collective_id=0, has_side_effects=True, vmem_limit_bytes=58 * 1024 * 1024
        ),
        cost_estimate=pl.CostEstimate(
            flops=13 * DEGREE * states * planes * width,
            bytes_accessed=4 * states * planes * width,
            transcendentals=0,
        ),
        name="filter_exchange",
    )(orbitals, potential, rotation)
    rows = n_st * states
    pieces = 4
    return pl.pallas_call(
        rotate_kernel,
        out_shape=jax.ShapeDtypeStruct((rows, points), jnp.bfloat16),
        in_specs=[anywhere] * 3,
        out_specs=anywhere,
        scratch_shapes=[
            pltpu.VMEM((rows, total), jnp.bfloat16),
            pltpu.VMEM((late, rows, width), jnp.bfloat16),
            pltpu.VMEM((late, rows, width), jnp.bfloat16),
            dma((late + 1,)), dma((pieces,)), dma((late,)),
        ],
        compiler_params=pltpu.CompilerParams(vmem_limit_bytes=60 * 1024 * 1024),
        cost_estimate=pl.CostEstimate(
            flops=2 * rows * total * late_points,
            bytes_accessed=4 * rows * points,
            transcendentals=0,
        ),
        name="rotate",
    )(rot_full.reshape(rows, total), gathered2, rotated1)


def solution(mesh):
    return jax.shard_map(
        functools.partial(local, mesh.shape["dom"], mesh.shape["st"]),
        mesh=mesh,
        in_specs=(P("st", "dom", None), P("dom", None), P("st", None)),
        out_specs=P(None, ("dom", "st")),
        check_vma=False,
    )
```

```python
import functools

import jax
import jax.numpy as jnp
from jax import lax
from jax.experimental import pallas as pl
from jax.experimental.pallas import tpu as pltpu
from jax.sharding import PartitionSpec as P

DEGREE = 4
NZ = 32
LANES = 128
ROWS = 16
GROUP = 4
MESH = pl.DeviceIdType.MESH

cheb_shift = 3.75
cheb_scale = 3.25


def filter_kernel(
    n_dom, n_st, parts,
    orb, pot, rot,
    gathered, rot_full,
    raw, halo, pot_v, pot_halo, alpha, y0, y1, y2, y3, stage,
    load_sem, pot_sem, halo_send, halo_recv, ph_send, ph_recv,
    send_sem, recv_sem, own_sem, r_send, r_recv, r_own, r2_send, r2_recv,
):
    dom = lax.axis_index("dom")
    me = lax.axis_index("st")
    states, planes, width = orb.shape
    chunks = states // ROWS
    block = planes // n_st
    half = n_st // 2
    cols = width // LANES
    part_rows = states // parts
    fields = (y0, y1, y2, y3)

    def load(c):
        return pltpu.make_async_copy(
            orb.at[pl.ds(c * ROWS, ROWS)], raw.at[pl.ds(c * ROWS, ROWS)], load_sem.at[c]
        )

    for c in range(chunks):
        load(c).start()
    pot_copy = pltpu.make_async_copy(pot, pot_v, pot_sem)
    pot_copy.start()

    barrier = pltpu.get_barrier_semaphore()
    for i in range(1, n_st):
        pl.semaphore_signal(
            barrier, inc=1, device_id={"st": lax.rem(me + i, n_st)}, device_id_type=MESH
        )
    for i in range(1, n_dom):
        pl.semaphore_signal(
            barrier, inc=1, device_id={"dom": lax.rem(dom + i, n_dom)}, device_id_type=MESH
        )

    lane = lax.broadcasted_iota(jnp.int32, (ROWS, LANES), 1)
    z_pos = lane % NZ

    for field in fields:
        field[pl.ds(0, DEGREE)] = jnp.zeros((DEGREE, ROWS, width), jnp.float32)
        field[pl.ds(planes + DEGREE, DEGREE)] = jnp.zeros((DEGREE, ROWS, width), jnp.float32)

    pl.semaphore_wait(barrier, n_st - 1 + n_dom - 1)

    def halo_copy(side, c):
        begin = planes - ROWS if side == 0 else 0
        target = jnp.clip(dom + 1 if side == 0 else dom - 1, 0, n_dom - 1)
        return pltpu.make_async_remote_copy(
            src_ref=orb.at[pl.ds(c * ROWS, ROWS), pl.ds(begin, ROWS)],
            dst_ref=halo.at[side, c],
            send_sem=halo_send.at[side, c],
            recv_sem=halo_recv.at[side, c],
            device_id={"dom": target},
            device_id_type=MESH,
        )

    def pot_halo_copy(side):
        begin = planes - ROWS if side == 0 else 0
        target = jnp.clip(dom + 1 if side == 0 else dom - 1, 0, n_dom - 1)
        return pltpu.make_async_remote_copy(
            src_ref=pot.at[pl.ds(begin, ROWS)],
            dst_ref=pot_halo.at[side],
            send_sem=ph_send.at[side],
            recv_sem=ph_recv.at[side],
            device_id={"dom": target},
            device_id_type=MESH,
        )

    has_next = dom < n_dom - 1
    has_prev = dom > 0
    sends_side = (has_next, has_prev)
    takes_side = (has_prev, has_next)

    for side in range(2):
        @pl.when(sends_side[side])
        def _():
            pot_halo_copy(side).start()
            for c in range(chunks):
                halo_copy(side, c).start()

    part = dom if parts > 1 else 0
    my_rows = rot.at[pl.ds(pl.multiple_of(part * part_rows, ROWS), part_rows)]

    def rot_copy(i, owner):
        return pltpu.make_async_remote_copy(
            src_ref=my_rows,
            dst_ref=rot_full.at[owner, part],
            send_sem=r_send.at[i],
            recv_sem=r_recv.at[owner],
            device_id={"st": lax.rem(me + i, n_st)},
            device_id_type=MESH,
        )

    for i in range(1, n_st):
        rot_copy(i, me).start()
    rot_own = pltpu.make_async_copy(my_rows, rot_full.at[me, part], r_own)
    rot_own.start()

    def set_alpha(source, source_row, q):
        row = 2.0 * (source.astype(jnp.float32) - (cheb_shift - 3.0))
        for i in range(ROWS):
            if source_row[0] <= i < source_row[1]:
                alpha[q + i - source_row[0]] = jnp.broadcast_to(row[i : i + 1], (8, width))

    pot_copy.wait()

    def alpha_rows(j, carry):
        set_alpha(pot_v[pl.ds(pl.multiple_of(j * ROWS, ROWS), ROWS)], (0, ROWS), DEGREE + j * ROWS)
        return carry

    lax.fori_loop(0, planes // ROWS, alpha_rows, 0)

    def turned(value):
        return jnp.swapaxes(value.astype(jnp.float32), 0, 1)

    def advance(count, k, q, c, b):
        source = fields[k - 1]
        zero = jnp.zeros((ROWS, LANES), jnp.float32)

        def rotate(i):
            at = pl.ds(i * LANES, LANES)
            ups, downs, sides = [], [], []
            for u in range(count):
                v = source[q + u, :, at]
                ups.append(pltpu.roll(v, LANES - NZ, 1))
                downs.append(pltpu.roll(v, NZ, 1))
                upper_z = jnp.where(z_pos < NZ - 1, pltpu.roll(v, LANES - 1, 1), 0.0)
                lower_z = jnp.where(z_pos > 0, pltpu.roll(v, 1, 1), 0.0)
                sides.append(upper_z + lower_z)
            return ups, downs, sides

        nothing = ([zero] * count,) * 3
        before, here = nothing, rotate(0)
        for i in range(cols):
            after = rotate(i + 1) if i + 1 < cols else nothing
            at = pl.ds(i * LANES, LANES)
            line = [source[q + u - 1, :, at] for u in range(count + 2)]
            results = []
            for u in range(count):
                upper_y = jnp.where(lane < LANES - NZ, here[0][u], after[0][u])
                lower_y = jnp.where(lane >= NZ, here[1][u], before[1][u])
                beside = (line[u + 2] + line[u]) + (upper_y + lower_y)
                beside = beside + here[2][u]
                a8 = alpha[q + u, :, at]
                applied = jnp.concatenate([a8] * (ROWS // 8), axis=0) * line[u + 1] - beside
                if k == 1:
                    result = applied * (0.5 / cheb_scale)
                else:
                    result = applied * (1.0 / cheb_scale) - fields[k - 2][q + u, :, at]
                results.append(result)
            for u in range(count):
                if k < DEGREE:
                    fields[k][q + u, :, at] = results[u]
                else:
                    offset = (q + u - DEGREE - b * block) * width + i * LANES
                    stage[c, b, :, pl.ds(pl.multiple_of(offset, LANES), LANES)] = results[
                        u
                    ].astype(jnp.bfloat16)
            before, here = here, after

    def send_copy(c, b):
        return pltpu.make_async_remote_copy(
            src_ref=stage.at[c, b],
            dst_ref=gathered.at[pl.ds(pl.multiple_of(me * states + c * ROWS, ROWS), ROWS)],
            send_sem=send_sem.at[c, b],
            recv_sem=recv_sem.at[c, me],
            device_id={"st": b},
            device_id_type=MESH,
        )

    def own_copy(c):
        return pltpu.make_async_copy(
            stage.at[c, me],
            gathered.at[pl.ds(pl.multiple_of(me * states + c * ROWS, ROWS), ROWS)],
            own_sem.at[c],
        )

    up_first = me < half
    odd = lax.rem(me, 2) if half > 1 else 0
    even = 1 - odd if half > 1 else 0
    pivot = jnp.where(up_first, half + odd, half - 1 - even)
    halo_blocks = -(-DEGREE // block)
    last = chunks - 1

    def block_at(step):
        upper = jnp.where(step < n_st - pivot, pivot + step, n_st - 1 - step)
        lower = jnp.where(step <= pivot, pivot - step, step)
        return jnp.where(up_first, upper, lower)

    def issue(c, b):
        @pl.when(b != me)
        def _():
            send_copy(c, b).start()

        @pl.when(b == me)
        def _():
            own_copy(c).start()

    def chunk_body(c, carry):
        load(c).wait()

        def turn(j, inner):
            at_planes = pl.ds(pl.multiple_of(j * ROWS, ROWS), ROWS)
            for i in range(cols):
                at = pl.ds(i * LANES, LANES)
                value = raw[pl.ds(pl.multiple_of(c * ROWS, ROWS), ROWS), at_planes, at]
                y0[pl.ds(DEGREE + j * ROWS, ROWS), :, at] = turned(value)
            return inner

        begin_row = jnp.maximum(pivot * block - DEGREE, 0) // ROWS
        end_row = jnp.minimum((pivot * block + block + DEGREE - 1) // ROWS + 1, planes // ROWS)

        def step_body(step, inner):
            b = block_at(step)
            up = jnp.where(
                up_first, (step < n_st - pivot).astype(jnp.int32), (step > pivot).astype(jnp.int32)
            )
            is_start = (step == 0).astype(jnp.int32)

            @pl.when(step == 0)
            def _():
                lax.fori_loop(begin_row, end_row, turn, 0)

            @pl.when(step == 1)
            def _():
                lax.fori_loop(0, begin_row, turn, 0)
                lax.fori_loop(end_row, planes // ROWS, turn, 0)

            for side in range(2):
                needed = n_st - halo_blocks if side else halo_blocks - 1

                @pl.when((b == needed) & (up == side) & takes_side[side])
                def _():
                    halo_copy(side, c).wait_recv()
                    begin = ROWS - DEGREE if side == 0 else 0
                    q = 0 if side == 0 else planes + DEGREE
                    for i in range(cols):
                        at = pl.ds(i * LANES, LANES)
                        y0[pl.ds(q, DEGREE), :, at] = turned(halo[side, c, :, :, at])[
                            begin : begin + DEGREE
                        ]

                    @pl.when(c == 0)
                    def _():
                        pot_halo_copy(side).wait_recv()
                        set_alpha(pot_halo[side], (begin, begin + DEGREE), q)

            for k in range(1, DEGREE + 1):
                reach = DEGREE - k
                low = b * block + DEGREE - reach + 2 * reach * up * (1 - is_start)
                high = b * block + block + DEGREE - reach + 2 * reach * jnp.maximum(up, is_start)
                low = jnp.maximum(low, jnp.where(has_prev, k, DEGREE))
                high = jnp.minimum(
                    high, jnp.where(has_next, planes + DEGREE + reach, planes + DEGREE)
                )

                groups = jnp.maximum(high - low, 0) // GROUP

                def group_body(t, nothing):
                    advance(GROUP, k, low + t * GROUP, c, b)
                    return nothing

                def plane_body(q, nothing):
                    advance(1, k, q, c, b)
                    return nothing

                lax.fori_loop(0, groups, group_body, 0)
                lax.fori_loop(low + groups * GROUP, high, plane_body, 0)

            if chunks == 1:
                issue(c, b)
            else:
                @pl.when((step < half) & (c > 0))
                def _():
                    issue(c - 1, block_at(step + half))

                @pl.when((step < half) & (c < last))
                def _():
                    issue(c, b)

                @pl.when((step >= half) & (c == last))
                def _():
                    issue(c, b)
                    issue(c, block_at(step - half))

            return inner

        lax.fori_loop(0, n_st, step_body, 0)
        return carry

    lax.fori_loop(0, chunks, chunk_body, 0)

    for i in range(1, n_st):
        rot_copy(i, lax.rem(me + i, n_st)).wait_recv()
    rot_own.wait()
    if parts > 1:
        def spread_copy(i, owner):
            return pltpu.make_async_remote_copy(
                src_ref=rot_full.at[:, owner],
                dst_ref=rot_full.at[:, owner],
                send_sem=r2_send.at[i],
                recv_sem=r2_recv.at[owner],
                device_id={"dom": lax.rem(dom + i, n_dom)},
                device_id_type=MESH,
            )

        for i in range(1, n_dom):
            spread_copy(i, dom).start()
        for i in range(1, n_dom):
            spread_copy(i, dom).wait_send()
            spread_copy(i, lax.rem(dom + i, n_dom)).wait_recv()
    for i in range(1, n_st):
        rot_copy(i, me).wait_send()
    for side in range(2):
        @pl.when(sends_side[side])
        def _():
            pot_halo_copy(side).wait_send()
            for c in range(chunks):
                halo_copy(side, c).wait_send()

    def arrival(c, i):
        peer = lax.rem(me + i, n_st)
        return pltpu.make_async_remote_copy(
            src_ref=stage.at[c, peer],
            dst_ref=gathered.at[pl.ds(pl.multiple_of(peer * states + c * ROWS, ROWS), ROWS)],
            send_sem=send_sem.at[c, peer],
            recv_sem=recv_sem.at[c, peer],
            device_id={"st": peer},
            device_id_type=MESH,
        )

    def finish(c, carry):
        def finish_peer(i, inner):
            arrival(c, i).wait_send()
            arrival(c, i).wait_recv()
            return inner

        lax.fori_loop(1, n_st, finish_peer, 0)
        own_copy(c).wait()
        return carry

    lax.fori_loop(0, chunks, finish, 0)


def rotate_kernel(rot, states, out):
    out[...] = jnp.dot(rot[...], states[...], preferred_element_type=jnp.float32).astype(out.dtype)


def local(n_dom, n_st, orbitals, potential, rotation):
    states, planes, width = orbitals.shape
    total = rotation.shape[1]
    chunks = states // ROWS
    block = planes // n_st
    points = block * width
    parts = n_dom if states % (ROWS * n_dom) == 0 else 1
    field = pltpu.VMEM((planes + 2 * DEGREE, ROWS, width), jnp.float32)
    dma = pltpu.SemaphoreType.DMA
    anywhere = pl.BlockSpec(memory_space=pl.ANY)
    gathered, rot_full = pl.pallas_call(
        functools.partial(filter_kernel, n_dom, n_st, parts),
        out_shape=(
            jax.ShapeDtypeStruct((n_st * states, points), jnp.bfloat16),
            jax.ShapeDtypeStruct((n_st, parts, states // parts, total), jnp.bfloat16),
        ),
        in_specs=[anywhere] * 3,
        out_specs=(anywhere, anywhere),
        scratch_shapes=[
            pltpu.VMEM((states, planes, width), jnp.bfloat16),
            pltpu.VMEM((2, chunks, ROWS, ROWS, width), jnp.bfloat16),
            pltpu.VMEM((planes, width), jnp.bfloat16),
            pltpu.VMEM((2, ROWS, width), jnp.bfloat16),
            pltpu.VMEM((planes + 2 * DEGREE, 8, width), jnp.float32),
            field, field, field, field,
            pltpu.VMEM((chunks, n_st, ROWS, points), jnp.bfloat16),
            dma((chunks,)), dma,
            dma((2, chunks)), dma((2, chunks)), dma((2,)), dma((2,)),
            dma((chunks, n_st)), dma((chunks, n_st)), dma((chunks,)),
            dma((n_st,)), dma((n_st,)), dma,
            dma((n_dom,)), dma((n_dom,)),
        ],
        compiler_params=pltpu.CompilerParams(
            collective_id=0, has_side_effects=True, vmem_limit_bytes=56 * 1024 * 1024
        ),
        cost_estimate=pl.CostEstimate(
            flops=13 * DEGREE * states * planes * width,
            bytes_accessed=4 * states * planes * width,
            transcendentals=0,
        ),
        name="filter_exchange",
    )(orbitals, potential, rotation)
    rot_all = rot_full.reshape(n_st * states, total)
    return pl.pallas_call(
        rotate_kernel,
        out_shape=jax.ShapeDtypeStruct((n_st * states, points), jnp.bfloat16),
        grid=(points // width,),
        in_specs=[
            pl.BlockSpec((n_st * states, total), lambda i: (0, 0)),
            pl.BlockSpec((n_st * states, width), lambda i: (0, i)),
        ],
        out_specs=pl.BlockSpec((n_st * states, width), lambda i: (0, i)),
        compiler_params=pltpu.CompilerParams(vmem_limit_bytes=60 * 1024 * 1024),
        cost_estimate=pl.CostEstimate(
            flops=2 * n_st * states * total * points,
            bytes_accessed=4 * n_st * states * points,
            transcendentals=0,
        ),
        name="rotate",
    )(rot_all, gathered)


def solution(mesh):
    return jax.shard_map(
        functools.partial(local, mesh.shape["dom"], mesh.shape["st"]),
        mesh=mesh,
        in_specs=(P("st", "dom", None), P("dom", None), P("st", None)),
        out_specs=P(None, ("dom", "st")),
        check_vma=False,
    )
```
